32 devices in a mesh: lat: 8 (over y, x, core), blk: 4 (over z).
Axes of the slice: x: 2, y: 2, z: 4, core: 2. Of those that a mesh axis runs over, the one named last changes fastest.
Arguments:
- tokens: float32 [8, 1024, 1152], P('lat', 'blk'), may hold values from -6 to 6
- condition: float32 [8, 1152], P('lat'), may hold values from -6 to 6
- cotangent: float32 [8, 1024, 1152], P('lat', 'blk'), may hold values from -6 to 6
- ada_weight: float32 [1152, 6912], P(('lat', 'blk')), may hold values from -0.1875 to 0.1875
- ada_bias: float32 [6912], P(('lat', 'blk')), may hold values from -2 to 2
- qkv_weight: float32 [1152, 3456], P(('lat', 'blk')), may hold values from -0.1875 to 0.1875
- query_bias: float32 [1152], P(('lat', 'blk')), may hold values from -3 to 3
- value_bias: float32 [1152], P(('lat', 'blk')), may hold values from -0.6 to 0.6
- proj_weight: float32 [1152, 1152], P(('lat', 'blk')), may hold values from -6 to 6
- proj_bias: float32 [1152], P(('lat', 'blk')), may hold values from -3 to 3
- up_weight: float32 [1152, 4608], P(('lat', 'blk')), may hold values from -0.1875 to 0.1875
- up_bias: float32 [4608], P(('lat', 'blk')), may hold values from -3 to 3
- down_weight: float32 [4608, 1152], P(('lat', 'blk')), may hold values from -0.09375 to 0.09375
- down_bias: float32 [1152], P(('lat', 'blk')), may hold values from -3 to 3
Outputs:
- output: float32 [8, 1024, 1152], P('lat', 'blk')
- grad_tokens: float32 [8, 1024, 1152], P('lat', 'blk')
- grad_condition: float32 [8, 1152], P('lat')
- grad_ada_weight: float32 [1152, 6912], P(('lat', 'blk'))
- grad_ada_bias: float32 [6912], P(('lat', 'blk'))
- grad_qkv_weight: float32 [1152, 3456], P(('lat', 'blk'))
- grad_query_bias: float32 [1152], P(('lat', 'blk'))
- grad_value_bias: float32 [1152], P(('lat', 'blk'))
- grad_proj_weight: float32 [1152, 1152], P(('lat', 'blk'))
- grad_proj_bias: float32 [1152], P(('lat', 'blk'))
- grad_up_weight: float32 [1152, 4608], P(('lat', 'blk'))
- grad_up_bias: float32 [4608], P(('lat', 'blk'))
- grad_down_weight: float32 [4608, 1152], P(('lat', 'blk'))
- grad_down_bias: float32 [1152], P(('lat', 'blk'))
The draws below stay inside these ranges and needn't reach their ends.
All inputs are finite; a program needn't handle non-finite values.
Results may differ from the reference program's by a relative error of at most 0.018.
The reference program's roundings to bfloat16 on the way count: a program that leaves them out, or rounds other values in their place, can miss the bound.
Values may be sent and summed in bfloat16 or wider, within the bound.
A program may use at most 320 MiB of HBM per device.

```python
import math
import jax
import jax.numpy as jnp
from jax import lax

D = 1152
H = 16
HD = 72
FF = 4608
SEQ = 1024
LATENTS = 8


def draw_ada_bias(key, part):
    base = 0.5 * jnp.clip(jax.random.normal(key, (6 * D,), jnp.float32), -4.0, 4.0)
    return base


def steps_of(rng, extent, pieces, low, high):
    level = 1.0
    for axis_at, shards_of in pieces:
        heights = jax.random.uniform(jax.random.fold_in(jax.random.fold_in(rng, 6), axis_at), (shards_of,), jnp.float32, low / len(pieces), high / len(pieces))
        level = level * jnp.repeat(jnp.exp(heights), extent[axis_at] // shards_of).reshape((-1,) + (1,) * (len(extent) - 1 - axis_at))
    return level


def bell_draw(key, extent, scale, bound, cuts=(), dtype=jnp.bfloat16):
    drawn = jax.random.normal(key, extent, jnp.float32) * scale
    if len(cuts) > 0:
        drawn = steps_of(key, extent, cuts, -0.22, 0.18) * drawn
    return jnp.clip(drawn, min=-bound, max=bound).astype(dtype)


def setup_inputs(seed: int = 0) -> dict:
    arg_keys = jax.random.split(jax.random.key(seed), 15)
    tokens = bell_draw(arg_keys[0], (LATENTS, SEQ, D), 1.0, 6.0, ((0, 8), (1, 4)), jnp.float32)
    condition = bell_draw(arg_keys[1], (LATENTS, D), 1.0, 6.0, ((0, 8),), jnp.float32)
    cotangent = bell_draw(arg_keys[2], (LATENTS, SEQ, D), 1.0, 6.0, ((0, 8), (1, 4)), jnp.float32)
    ada_weight = bell_draw(arg_keys[3], (D, 6 * D), D ** -0.5, 0.1875, ((0, 32),), jnp.float32)
    ada_bias = draw_ada_bias(jax.random.fold_in(arg_keys[14], 71), 0)
    qkv_weight = bell_draw(arg_keys[5], (D, 3 * D), D ** -0.5, 0.1875, ((0, 32),), jnp.float32)
    query_bias = bell_draw(arg_keys[6], (D,), 0.5, 3.0, ((0, 32),), jnp.float32)
    value_bias = bell_draw(arg_keys[7], (D,), 0.1, 0.6, ((0, 32),), jnp.float32)
    proj_weight = bell_draw(arg_keys[8], (D, D), (max(1, D // SEQ)) ** -0.5, 6.0, ((0, 32),), jnp.float32)
    proj_bias = bell_draw(arg_keys[9], (D,), 0.5, 3.0, ((0, 32),), jnp.float32)
    up_weight = bell_draw(arg_keys[10], (D, FF), D ** -0.5, 0.1875, ((0, 32),), jnp.float32)
    up_bias = bell_draw(arg_keys[11], (FF,), 0.5, 3.0, ((0, 32),), jnp.float32)
    down_weight = bell_draw(arg_keys[12], (FF, D), FF ** -0.5, 0.09375, ((0, 32),), jnp.float32)
    down_bias = bell_draw(arg_keys[13], (D,), 0.5, 3.0, ((0, 32),), jnp.float32)
    return {"tokens": tokens, "condition": condition, "cotangent": cotangent, "ada_weight": ada_weight, "ada_bias": ada_bias, "qkv_weight": qkv_weight, "query_bias": query_bias, "value_bias": value_bias, "proj_weight": proj_weight, "proj_bias": proj_bias, "up_weight": up_weight, "up_bias": up_bias, "down_weight": down_weight, "down_bias": down_bias}


EPS = 1e-06
GELU_C = 0.7978845608028654
CUBIC = 0.044715
HIGH = lax.Precision.HIGHEST

def rounded(value):
    return lax.optimization_barrier(value.astype(jnp.bfloat16)).astype(jnp.float32)

def layer_norm(value):
    mean = lax.optimization_barrier(jnp.mean(value, axis=-1, keepdims=True))
    centered = value - mean
    rstd = lax.rsqrt(lax.optimization_barrier(jnp.mean(centered * centered, axis=-1, keepdims=True)) + EPS)
    return (centered * rstd, rstd)

def norm_back(grad, normed, rstd):
    return (grad - lax.optimization_barrier(jnp.mean(grad, axis=-1, keepdims=True)) - normed * lax.optimization_barrier(jnp.mean(grad * normed, axis=-1, keepdims=True))) * rstd

def gelu_tanh(value):
    return 0.5 * value * (1.0 + jnp.tanh(GELU_C * (value + CUBIC * value * value * value)))

def gelu_slope(value):
    inner = jnp.tanh(GELU_C * (value + CUBIC * value * value * value))
    return 0.5 * (1.0 + inner) + 0.5 * value * (1.0 - inner * inner) * GELU_C * (1.0 + 3.0 * CUBIC * value * value)

def silu_slope(value):
    sigma = jax.nn.sigmoid(value)
    return sigma * (1.0 + value * (1.0 - sigma))

def one_latent(weights, tokens, condition, cotangent):
    ada_weight, ada_bias, qkv_weight, query_bias, value_bias, proj_weight, proj_bias, up_weight, up_bias, down_weight, down_bias = weights
    scale = 1.0 / math.sqrt(HD)
    cond_act = jax.nn.silu(condition)
    modulation = jnp.dot(cond_act.astype(jnp.bfloat16)[None, :], ada_weight, preferred_element_type=jnp.float32)[0] + ada_bias.astype(jnp.float32)
    shift1, scale1, gate1, shift2, scale2, gate2 = jnp.split(modulation, 6)
    normed1, rstd1 = layer_norm(tokens)
    attn_in = (normed1 * (1.0 + scale1) + shift1).astype(jnp.bfloat16)
    offsets = jnp.concatenate([query_bias, jnp.zeros_like(query_bias), value_bias]).astype(jnp.float32)
    qkv = (jnp.dot(attn_in, qkv_weight, preferred_element_type=jnp.float32) + offsets).astype(jnp.bfloat16)
    query = qkv[:, :D].reshape(SEQ, H, HD).astype(jnp.float32)
    keys = qkv[:, D:2 * D].reshape(SEQ, H, HD).astype(jnp.float32)
    values = qkv[:, 2 * D:].reshape(SEQ, H, HD).astype(jnp.float32)
    scores = jnp.einsum('qhd,khd->hqk', query, keys) * scale
    peak = lax.optimization_barrier(jnp.max(scores, axis=-1, keepdims=True))
    expo = jnp.exp(scores - peak)
    total = lax.optimization_barrier(jnp.sum(expo, axis=-1, keepdims=True))
    log_total = peak + jnp.log(total)
    mixed = jnp.einsum('hqk,khd->hqd', rounded(expo), values) / total
    attn = mixed.transpose(1, 0, 2).reshape(SEQ, D).astype(jnp.bfloat16)
    proj = jnp.dot(attn, proj_weight, preferred_element_type=jnp.float32) + proj_bias.astype(jnp.float32)
    mid = tokens + gate1 * proj
    normed2, rstd2 = layer_norm(mid)
    mlp_in = (normed2 * (1.0 + scale2) + shift2).astype(jnp.bfloat16)
    hidden = jnp.dot(mlp_in, up_weight, preferred_element_type=jnp.float32) + up_bias.astype(jnp.float32)
    act = gelu_tanh(hidden).astype(jnp.bfloat16)
    mlp_out = jnp.dot(act, down_weight, preferred_element_type=jnp.float32) + down_bias.astype(jnp.float32)
    output = mid + gate2 * mlp_out
    grad_gate2 = lax.optimization_barrier(jnp.sum(cotangent * mlp_out, axis=0))
    d_mlp = cotangent * gate2
    d_mlp16 = d_mlp.astype(jnp.bfloat16)
    grad_down_weight = jnp.dot(act.T, d_mlp16, preferred_element_type=jnp.float32)
    grad_down_bias = lax.optimization_barrier(jnp.sum(d_mlp, axis=0))
    d_hidden = jnp.dot(d_mlp16, down_weight.T, preferred_element_type=jnp.float32) * gelu_slope(hidden)
    d_hidden16 = d_hidden.astype(jnp.bfloat16)
    grad_up_weight = jnp.dot(mlp_in.T, d_hidden16, preferred_element_type=jnp.float32)
    grad_up_bias = lax.optimization_barrier(jnp.sum(d_hidden, axis=0))
    d_mlp_in = jnp.dot(d_hidden16, up_weight.T, preferred_element_type=jnp.float32)
    grad_shift2 = lax.optimization_barrier(jnp.sum(d_mlp_in, axis=0))
    grad_scale2 = lax.optimization_barrier(jnp.sum(d_mlp_in * normed2, axis=0))
    d_mid = cotangent + norm_back(d_mlp_in * (1.0 + scale2), normed2, rstd2)
    grad_gate1 = lax.optimization_barrier(jnp.sum(d_mid * proj, axis=0))
    d_proj = d_mid * gate1
    d_proj16 = d_proj.astype(jnp.bfloat16)
    grad_proj_weight = jnp.dot(attn.T, d_proj16, preferred_element_type=jnp.float32)
    grad_proj_bias = lax.optimization_barrier(jnp.sum(d_proj, axis=0))
    d_attn = jnp.dot(d_proj16, proj_weight.T, preferred_element_type=jnp.float32).astype(jnp.bfloat16)
    d_attn3 = d_attn.reshape(SEQ, H, HD).astype(jnp.float32)
    attn3 = attn.reshape(SEQ, H, HD).astype(jnp.float32)
    delta = lax.optimization_barrier(jnp.sum(d_attn3 * attn3, axis=-1)).T[:, :, None]
    probs = jnp.exp(scores - log_total)
    d_values = jnp.einsum('hqk,qhd->khd', rounded(probs), d_attn3)
    d_probs = jnp.einsum('qhd,khd->hqk', d_attn3, values)
    d_scores = rounded(probs * (d_probs - delta) * scale)
    d_query = jnp.einsum('hqk,khd->qhd', d_scores, keys).reshape(SEQ, D)
    d_keys = jnp.einsum('hqk,qhd->khd', d_scores, query).reshape(SEQ, D)
    d_values = d_values.reshape(SEQ, D)
    d_qkv = jnp.concatenate([d_query, d_keys, d_values], axis=-1).astype(jnp.bfloat16)
    grad_qkv_weight = jnp.dot(attn_in.T, d_qkv, preferred_element_type=jnp.float32)
    grad_query_bias = lax.optimization_barrier(jnp.sum(d_query, axis=0))
    grad_value_bias = lax.optimization_barrier(jnp.sum(d_values, axis=0))
    d_attn_in = jnp.dot(d_qkv, qkv_weight.T, preferred_element_type=jnp.float32)
    grad_shift1 = lax.optimization_barrier(jnp.sum(d_attn_in, axis=0))
    grad_scale1 = lax.optimization_barrier(jnp.sum(d_attn_in * normed1, axis=0))
    grad_tokens = d_mid + norm_back(d_attn_in * (1.0 + scale1), normed1, rstd1)
    d_mod = jnp.concatenate([grad_shift1, grad_scale1, grad_gate1, grad_shift2, grad_scale2, grad_gate2])
    grad_ada_weight = jnp.outer(cond_act, d_mod)
    grad_condition = jnp.dot(d_mod, ada_weight.astype(jnp.float32).T, precision=HIGH) * silu_slope(condition)
    grads = (grad_ada_weight, d_mod, grad_qkv_weight, grad_query_bias, grad_value_bias, grad_proj_weight, grad_proj_bias, grad_up_weight, grad_up_bias, grad_down_weight, grad_down_bias)
    return (output, grad_tokens, grad_condition, grads)

def reference(tokens, condition, cotangent, ada_weight, ada_bias, qkv_weight, query_bias, value_bias, proj_weight, proj_bias, up_weight, up_bias, down_weight, down_bias):
    weights = tuple((weight.astype(jnp.bfloat16) for weight in (ada_weight, ada_bias, qkv_weight, query_bias, value_bias, proj_weight, proj_bias, up_weight, up_bias, down_weight, down_bias)))

    def step(carry, inputs):
        output, grad_tokens, grad_condition, grads = one_latent(weights, inputs[0], inputs[1], inputs[2])
        carry = tuple((left + right for left, right in zip(carry, grads)))
        return (carry, (output, grad_tokens, grad_condition))
    zeros = tuple((jnp.zeros(weight.shape, jnp.float32) for weight in weights))
    sums, stacked = lax.scan(step, zeros, (tokens, condition, cotangent))
    return (stacked[0], stacked[1], stacked[2], sums[0], sums[1], sums[2], sums[3], sums[4], sums[5], sums[6], sums[7], sums[8], sums[9], sums[10])
```

```python
import math

import jax
import jax.numpy as jnp
from jax import lax
from jax.experimental import pallas as pl
from jax.experimental.pallas import tpu as pltpu
from jax.sharding import PartitionSpec as P

H = 16
EPS = 1e-06
GELU_C = 0.7978845608028654
CUBIC = 0.044715
HIGH = lax.Precision.HIGHEST
BOTH = ("lat", "blk")
F32 = jnp.float32
BF16 = jnp.bfloat16


def layer_norm(value):
    mean = jnp.mean(value, axis=-1, keepdims=True)
    centered = value - mean
    rstd = lax.rsqrt(jnp.mean(centered * centered, axis=-1, keepdims=True) + EPS)
    return (centered * rstd, rstd)


def norm_back(grad, normed, rstd):
    return (
        grad
        - jnp.mean(grad, axis=-1, keepdims=True)
        - normed * jnp.mean(grad * normed, axis=-1, keepdims=True)
    ) * rstd


def silu_slope(value):
    sigma = jax.nn.sigmoid(value)
    return sigma * (1.0 + value * (1.0 - sigma))


def dot(left, right):
    return jnp.dot(left, right, preferred_element_type=F32)


def dot_nt(left, right):
    return lax.dot_general(left, right, (((1,), (1,)), ((), ())), preferred_element_type=F32)


def dot_tn(left, right):
    return lax.dot_general(left, right, (((0,), (0,)), ((), ())), preferred_element_type=F32)


def scatter_rows(term, n):
    pieces = term.astype(BF16).reshape(n, term.shape[0] // n, term.shape[1])
    return lax.psum_scatter(pieces, BOTH, scatter_dimension=0).astype(F32)


MESH = pl.DeviceIdType.MESH
VMEM = pltpu.VMEM


def flip(index, bit):
    return index + bit - 2 * bit * ((index // bit) % 2)


def place(bias_ref, start, total):
    count = bias_ref.shape[1]
    row = lax.broadcasted_iota(jnp.int32, (count, total), 0)
    col = lax.broadcasted_iota(jnp.int32, (count, total), 1)
    spot = jnp.where(col == row + start, 1.0, 0.0).astype(BF16)
    return dot(bias_ref[...].astype(BF16), spot)


class Spread:
    def __init__(self, full, own, rows, halves, sems, l, z):
        self.full, self.own, self.rows, self.halves = full, own, rows, halves
        self.send, self.recv = sems
        self.l, self.z = l, z
        self.lx, self.ly, self.lc = flip(l, 2), flip(l, 4), flip(l, 1)
        self.lxy = flip(self.lx, 4)

    def view(self, lat, half=None):
        start = pl.multiple_of(lat * self.rows, 16)
        if half is None:
            return self.full.at[pl.ds(start, self.rows), :]
        (row, row_count), (col, col_count) = self.halves[half]
        return self.full.at[pl.ds(pl.multiple_of(start + row, 16), row_count), pl.ds(col, col_count)]

    def copy(self, k, src, dst, to):
        return pltpu.make_async_remote_copy(
            src_ref=src,
            dst_ref=dst,
            send_sem=self.send.at[k],
            recv_sem=self.recv.at[k],
            device_id=(to, self.z),
            device_id_type=MESH,
        )

    def out(self, k):
        l, lx, ly, lc, lxy = self.l, self.lx, self.ly, self.lc, self.lxy
        own = self.own
        return [
            lambda: self.copy(0, own, self.view(l), lx),
            lambda: self.copy(1, own, self.view(l), ly),
            lambda: self.copy(2, self.view(lx, 0), self.view(lx, 0), ly),
            lambda: self.copy(3, self.view(ly, 1), self.view(ly, 1), lx),
            lambda: self.copy(4, own, self.view(l), lc),
            lambda: self.copy(5, self.view(lx), self.view(lx), lc),
            lambda: self.copy(6, self.view(ly), self.view(ly), lc),
            lambda: self.copy(7, self.view(lxy, 0), self.view(lxy, 0), lc),
            lambda: self.copy(8, self.view(lxy, 1), self.view(lxy, 1), lc),
        ][k]()

    def arrival(self, k):
        lx, ly, lc, lxy = self.lx, self.ly, self.lc, self.lxy
        lat, half, sender = [
            (lx, None, lx),
            (ly, None, ly),
            (lxy, 0, ly),
            (lxy, 1, lx),
            (lc, None, lc),
            (flip(lc, 2), None, lc),
            (flip(lc, 4), None, lc),
            (flip(flip(lc, 2), 4), 0, lc),
            (flip(flip(lc, 2), 4), 1, lc),
        ][k]
        here = self.view(lat, half)
        return self.copy(k, here, here, sender)

    def start(self):
        for k in (0, 1, 4):
            self.out(k).start()

    def pass_x(self):
        self.arrival(0).wait_recv()
        self.out(2).start()
        self.out(5).start()

    def pass_y(self):
        self.arrival(1).wait_recv()
        self.out(3).start()
        self.out(6).start()

    def pass_core(self):
        self.arrival(2).wait_recv()
        self.out(7).start()
        self.arrival(3).wait_recv()
        self.out(8).start()

    def finish(self):
        for k in range(4, 9):
            self.arrival(k).wait_recv()

    def drain(self):
        for k in range(9):
            self.out(k).wait_send()


def forward_kernel(
    cond_ref, tokens_ref, ada_ref, qkv_ref, proj_ref, up_ref, down_ref,
    ada_b, q_b, v_b, p_b, d_b, u_b,
    vec_out, cond_out, up_full, down_full, proj_full, qkv_full, in_all, q_out, k_out, v_out, mixed_out, lse_out, attn_out,
    act_s, part, part_in, mod_z, normed_s, wide_s, qkv_s, qkv_z, proj_s, proj_z, up_s, up_z, up_own, proj_own, down_s, turned, joined,
    sem_a, sem_b, sem_c, sem_z, sem_in, sem_at, sem_send, sem_recv, sem_l,
):
    l, z = lax.axis_index("lat"), lax.axis_index("blk")
    nl, nb = cond_out.shape[0], in_all.shape[0]
    index = l * nb + z
    width = tokens_ref.shape[1]
    rows = tokens_ref.shape[0]
    share = proj_ref.shape[0]
    local = width // nb
    size = width // H
    heads = H // nb
    hidden_size = up_ref.shape[1]
    column = nb * share
    scale = 1.0 / math.sqrt(size)

    def lat_at(distance):
        at = l
        for bit in (1, 2, 4):
            if distance & bit:
                at = flip(at, bit)
        return at

    def blk_at(step):
        return lax.rem(z + step, nb)

    def remote(src, dst, send, recv, lat, blk):
        return pltpu.make_async_remote_copy(
            src_ref=src, dst_ref=dst, send_sem=send, recv_sem=recv, device_id=(lat, blk), device_id_type=MESH
        )

    barrier = pltpu.get_barrier_semaphore()
    for d in range(1, nl):
        pl.semaphore_signal(barrier, inc=1, device_id=(lat_at(d), z), device_id_type=MESH)
    for j in range(1, nb):
        pl.semaphore_signal(barrier, inc=1, device_id=(l, blk_at(j)), device_id_type=MESH)
    pl.semaphore_wait(barrier, nl + nb - 2)

    cond = cond_ref[...]
    cond_act = cond / (1.0 + jnp.exp(-cond))
    act_s[...] = cond_act
    cond_out[l] = cond_act
    cond_copies = [
        remote(act_s, cond_out.at[l], sem_a.at[0, d], sem_a.at[1, d], lat_at(d), z) for d in range(1, nl)
    ]
    for copy in cond_copies:
        copy.start()

    for b in range(nb):
        for third in range(3):
            at = third * width + b * local
            qkv_s[b, 0:share, third * local : (third + 1) * local] = qkv_ref[:, at : at + local].astype(BF16)
    proj_s[0:share, :] = proj_ref[...].astype(BF16)
    down_s[...] = down_ref[...].astype(BF16)
    for c in range(hidden_size // width):
        wide_s[c * share : (c + 1) * share, 0:width] = up_ref[:, c * width : (c + 1) * width]
    up_s[...] = wide_s[:, 0:width].astype(BF16)

    def blk_copies(k, src_of, dst_of):
        out, come = [], []
        for j in range(1, nb):
            to, sender = blk_at(j), blk_at(nb - j)
            out.append(remote(src_of(to), dst_of(z), sem_z.at[0, k, j], sem_z.at[1, k, j], l, to))
            come.append(remote(src_of(to), dst_of(sender), sem_z.at[0, k, j], sem_z.at[1, k, j], l, sender))
        return out, come

    down_start = l * (nb * down_s.shape[0])

    def down_slot(b):
        start = pl.multiple_of(down_start + b * down_s.shape[0], 16)
        return down_full.at[pl.ds(start, down_s.shape[0]), :]

    qkv_out_z, qkv_in_z = blk_copies(0, lambda to: qkv_s.at[to], lambda b: qkv_z.at[b])
    proj_out_z, proj_in_z = blk_copies(1, lambda to: proj_s, lambda b: proj_z.at[b])
    up_out_z, up_in_z = blk_copies(2, lambda to: up_s, lambda b: up_z.at[b])
    down_out_z, down_in_z = blk_copies(3, lambda to: down_s, down_slot)
    for copy in qkv_out_z + proj_out_z + up_out_z:
        copy.start()
    own_down = pltpu.make_async_copy(down_s, down_slot(z), sem_l.at[0])
    own_down.start()
    qkv_z[z] = qkv_s[z]
    proj_z[z] = proj_s[...]
    up_z[z] = up_s[...]

    offsets = jnp.concatenate(
        [place(ada_b, index * ada_b.shape[1], 6 * width)]
        + [place(b, index * share, width) for b in (q_b, v_b, p_b, d_b)]
        + [place(u_b, index * u_b.shape[1], hidden_size)],
        axis=1,
    )

    lanes = lax.broadcasted_iota(jnp.int32, (nl, width), 0)
    for d in range(1, nl):
        remote(act_s, cond_out.at[lat_at(d)], sem_a.at[0, d], sem_a.at[1, d], lat_at(d), z).wait_recv()
    every = jnp.zeros((nl, width), F32)
    for i in range(nl):
        every = jnp.where(lanes == i, jnp.broadcast_to(cond_out[i], (nl, width)), every)
    row = lax.broadcasted_iota(jnp.int32, (width, share), 0)
    col = lax.broadcasted_iota(jnp.int32, (width, share), 1)
    pick = jnp.where(row == col + index * share, 1.0, 0.0).astype(BF16)
    picked = dot(every.astype(BF16), pick).astype(BF16)
    product = dot(picked, ada_ref[...].astype(BF16))
    for i in range(nl):
        part[i, :, 0 : 6 * width] = product[i : i + 1, :] + offsets[:, 0 : 6 * width]
        part[i, :, 6 * width :] = offsets[:, 6 * width :]
    part_copies = []
    for d in range(1, nl):
        to = lat_at(d)
        part_copies.append(remote(part.at[to], part_in.at[l], sem_b.at[0, d], sem_b.at[1, d], to, z))
        part_copies[-1].start()
    part_in[l] = part[l]

    value = tokens_ref[...]
    centered = value - jnp.mean(value, axis=-1, keepdims=True)
    normed_s[...] = centered * lax.rsqrt(jnp.mean(centered * centered, axis=-1, keepdims=True) + EPS)

    for d in range(1, nl):
        remote(part.at[l], part_in.at[lat_at(d)], sem_b.at[0, d], sem_b.at[1, d], lat_at(d), z).wait_recv()
    total = part_in[0]
    for i in range(1, nl):
        total = total + part_in[i]
    mod_z[z] = total
    mod_copies = []
    for j in range(1, nb):
        mod_copies.append(remote(mod_z.at[z], mod_z.at[z], sem_c.at[0, j], sem_c.at[1, j], l, blk_at(j)))
        mod_copies[-1].start()

    def gather_column(slots, wide, dst, at):
        for b in range(nb):
            wide_s[b * share : (b + 1) * share, 0:wide] = slots[b].astype(F32)[0:share, :]
        dst[at, :] = wide_s[:, 0:wide].astype(BF16)

    whole = slice(None)
    mine = pl.ds(pl.multiple_of(l * column, 16), column)

    def sems(w):
        return sem_send.at[w], sem_recv.at[w]

    low = column // 32 * 16 + 16 if column % 32 else column // 2
    rows_low = (((0, low), (0, width)), ((low, column - low), (0, width)))
    rows_high = (((0, column - low), (0, 3 * local)), ((column - low, low), (0, 3 * local)))
    half = hidden_size // 2
    tall = nb * down_s.shape[0]
    spread_qkv = Spread(qkv_full, qkv_full.at[mine, :], column, rows_high, sems(0), l, z)
    spread_proj = Spread(proj_full, proj_own, column, rows_low, sems(1), l, z)
    spread_up = Spread(up_full, up_own, column, (((0, column), (0, half)), ((0, column), (half, half))), sems(2), l, z)
    spread_down = Spread(
        down_full,
        down_full.at[pl.ds(pl.multiple_of(down_start, 16), tall), :],
        tall,
        (((0, tall // 2), (0, width)), ((tall // 2, tall // 2), (0, width))),
        sems(3),
        l,
        z,
    )

    for copy in qkv_in_z:
        copy.wait_recv()
    gather_column(qkv_z, 3 * local, qkv_full, mine)
    spread_qkv.start()
    for copy in proj_in_z:
        copy.wait_recv()
    gather_column(proj_z, width, proj_own, whole)
    spread_proj.start()
    own_proj = pltpu.make_async_copy(proj_own, proj_full.at[mine, :], sem_l.at[1])
    own_proj.start()

    for j in range(1, nb):
        sender = blk_at(nb - j)
        remote(mod_z.at[sender], mod_z.at[sender], sem_c.at[0, j], sem_c.at[1, j], l, sender).wait_recv()
    vec = mod_z[0]
    for b in range(1, nb):
        vec = vec + mod_z[b]
    vec_out[...] = vec
    in_all[z] = (normed_s[...] * (1.0 + vec[:, width : 2 * width]) + vec[:, 0:width]).astype(BF16)
    in_out, in_in = [], []
    for j in range(1, nb):
        to, sender = blk_at(j), blk_at(nb - j)
        in_out.append(remote(in_all.at[z], in_all.at[z], sem_in.at[0, j], sem_in.at[1, j], l, to))
        in_in.append(remote(in_all.at[sender], in_all.at[sender], sem_in.at[0, j], sem_in.at[1, j], l, sender))
        in_out[-1].start()
    for copy in down_out_z:
        copy.start()

    for copy in up_in_z:
        copy.wait_recv()
    for c in range(hidden_size // width):
        for b in range(nb):
            wide_s[b * share : (b + 1) * share, 0:width] = up_z[b].astype(F32)[c * share : (c + 1) * share, :]
        up_own[:, c * width : (c + 1) * width] = wide_s[:, 0:width].astype(BF16)
    spread_up.start()
    own_up = pltpu.make_async_copy(up_own, up_full.at[mine, :], sem_l.at[2])
    own_up.start()

    spread_qkv.pass_x()
    spread_qkv.pass_y()
    spread_qkv.pass_core()
    spread_qkv.finish()

    q_off = jnp.zeros((1, local), F32)
    v_off = jnp.zeros((1, local), F32)
    for b in range(nb):
        at = 6 * width + b * local
        q_off = jnp.where(z == b, vec[:, at : at + local], q_off)
        v_off = jnp.where(z == b, vec[:, at + width : at + width + local], v_off)
    shift = jnp.concatenate([q_off, jnp.zeros((1, local), F32), v_off], axis=1)

    def project(b):
        block = dot(in_all[b], qkv_full[...]) + shift
        for h in range(heads):
            at = h * size
            q_out[h, b] = block[:, at : at + size].astype(BF16)
            k_out[h, b] = block[:, local + at : local + at + size].astype(BF16)
            value = block[:, 2 * local + at : 2 * local + at + size]
            v_out[h, b] = value.astype(BF16)
            turned[h, b] = value.T.astype(BF16)

    project(z)
    spread_proj.pass_x()
    spread_proj.pass_y()
    for j in range(1, nb):
        in_in[j - 1].wait_recv()
        project(blk_at(nb - j))
    spread_up.pass_x()
    spread_up.pass_y()
    own_down.wait()
    for copy in down_in_z:
        copy.wait_recv()
    spread_down.start()

    factor = scale * 1.4426950408889634

    def attend(step, carry):
        j, h = step // heads, lax.rem(step, heads)
        b = lax.rem(z + 1 + j, nb)
        keys = k_out[h].reshape(nb * rows, size)
        raw = dot_nt(keys, q_out[h, b])
        top = jnp.max(raw, axis=0, keepdims=True)
        expo = jnp.exp2(raw * factor - top * factor)
        norm = jnp.sum(expo, axis=0, keepdims=True)
        lse_out[h, b] = top * scale + jnp.log(norm)
        expo16 = expo.astype(BF16)
        mixed = dot(turned[h, 0], expo16[0:rows])
        for other in range(1, nb):
            mixed = mixed + dot(turned[h, other], expo16[other * rows : (other + 1) * rows])
        mixed_out[h, b] = (mixed / norm).T.astype(BF16)
        return carry

    lax.fori_loop(0, nb * heads, attend, 0)
    for j in range(nb):
        b = lax.rem(z + 1 + j, nb)
        for h in range(heads):
            joined[b, :, h * size : (h + 1) * size] = mixed_out[h, b]
        if j < nb - 1:
            remote(joined.at[b], attn_out.at[z], sem_at.at[0, j], sem_at.at[1, j], l, b).start()
    attn_out[z] = joined[z]

    spread_proj.pass_core()
    spread_up.pass_core()
    spread_down.pass_x()
    spread_down.pass_y()
    spread_down.pass_core()
    own_up.wait()
    own_proj.wait()
    for j in range(nb - 1):
        sender = blk_at(nb - 1 - j)
        remote(joined.at[z], attn_out.at[sender], sem_at.at[0, j], sem_at.at[1, j], l, sender).wait_recv()
    for spread in (spread_proj, spread_up, spread_down):
        spread.finish()
    for spread in (spread_qkv, spread_proj, spread_up, spread_down):
        spread.drain()
    for copy in cond_copies + part_copies + mod_copies + in_out:
        copy.wait_send()
    for copy in qkv_out_z + proj_out_z + up_out_z + down_out_z:
        copy.wait_send()
    for j in range(nb - 1):
        to = blk_at(1 + j)
        remote(joined.at[to], attn_out.at[z], sem_at.at[0, j], sem_at.at[1, j], l, to).wait_send()


def forward(nl, nb, tokens, condition, weights, biases):
    ada, qkv, proj, up, down = weights
    rows, width = tokens.shape
    share, hidden_size, down_rows = proj.shape[0], up.shape[1], down.shape[0]
    local, heads, column, size = width // nb, H // nb, nb * share, width // H
    pad = -(-share // 16) * 16
    total = 6 * width + 4 * width + hidden_size
    sd = jax.ShapeDtypeStruct
    in_vmem, in_hbm = pl.BlockSpec(memory_space=VMEM), pl.BlockSpec(memory_space=pl.ANY)
    outs = [
        (sd((1, total), F32), in_vmem),
        (sd((nl, 1, width), F32), in_vmem),
        (sd((width, hidden_size), BF16), in_hbm),
        (sd((hidden_size, width), BF16), in_hbm),
        (sd((width, width), BF16), in_hbm),
        (sd((width, 3 * local), BF16), in_vmem),
        (sd((nb, rows, width), BF16), in_vmem),
        (sd((heads, nb, rows, size), BF16), in_vmem),
        (sd((heads, nb, rows, size), BF16), in_vmem),
        (sd((heads, nb, rows, size), BF16), in_vmem),
        (sd((heads, nb, rows, size), BF16), in_vmem),
        (sd((heads, nb, 1, rows), F32), in_vmem),
        (sd((nb, rows, local), BF16), in_vmem),
    ]
    dma = pltpu.SemaphoreType.DMA
    scratch = [
        VMEM((1, width), F32),
        VMEM((nl, 1, total), F32),
        VMEM((nl, 1, total), F32),
        VMEM((nb, 1, total), F32),
        VMEM((rows, width), F32),
        VMEM((column, width), F32),
        VMEM((nb, pad, 3 * local), BF16),
        VMEM((nb, pad, 3 * local), BF16),
        VMEM((pad, width), BF16),
        VMEM((nb, pad, width), BF16),
        VMEM((share * hidden_size // width, width), BF16),
        VMEM((nb, share * hidden_size // width, width), BF16),
        VMEM((column, hidden_size), BF16),
        VMEM((column, width), BF16),
        VMEM((down_rows, width), BF16),
        VMEM((heads, nb, size, rows), BF16),
        VMEM((nb, rows, local), BF16),
        dma((2, nl)),
        dma((2, nl)),
        dma((2, nb)),
        dma((2, 4, nb)),
        dma((2, nb)),
        dma((2, nb)),
        dma((4, 9)),
        dma((4, 9)),
        dma((3,)),
    ]
    args = [condition, tokens, ada, qkv, proj, up, down] + [bias.reshape(1, -1) for bias in biases]
    return pl.pallas_call(
        forward_kernel,
        out_shape=[shape for shape, _ in outs],
        in_specs=[in_vmem] * len(args),
        out_specs=[spec for _, spec in outs],
        scratch_shapes=scratch,
        compiler_params=pltpu.CompilerParams(
            collective_id=0, has_side_effects=True, vmem_limit_bytes=56 * 2**20
        ),
        name="forward",
    )(*args)


def fused(
    tokens,
    condition,
    cotangent,
    ada_weight,
    ada_bias,
    qkv_weight,
    query_bias,
    value_bias,
    proj_weight,
    proj_bias,
    up_weight,
    up_bias,
    down_weight,
    down_bias,
):
    tokens, cotangent = tokens[0], cotangent[0]
    rows, width = tokens.shape
    nb, nl = lax.axis_size("blk"), lax.axis_size("lat")
    n = nb * nl
    my_lat, my_blk = lax.axis_index("lat"), lax.axis_index("blk")
    index = my_lat * nb + my_blk
    hidden_size = up_weight.shape[1]
    share = width // n
    heads = H // nb
    size = width // H
    local = heads * size
    seq = rows * nb
    scale = 1.0 / math.sqrt(size)

    weights = (ada_weight, qkv_weight, proj_weight, up_weight, down_weight)
    biases = (ada_bias, query_bias, value_bias, proj_bias, down_bias, up_bias)
    vec, cond_all, up_matrix, down_matrix, out_matrix, qkv_cols, in_all, query, keys, values, mixed, lse, attn = forward(
        nl, nb, tokens, condition, weights, biases
    )
    shift1, scale1, gate1, shift2, scale2, gate2 = [vec[:, i * width : (i + 1) * width] for i in range(6)]
    out_off, down_off = [vec[:, i * width : (i + 1) * width] for i in (8, 9)]
    up_off = vec[:, 10 * width :]
    picked = lax.dynamic_slice_in_dim(cond_all[:, 0], index * share, share, axis=1)
    ada16 = ada_weight.astype(BF16)
    normed1, rstd1 = layer_norm(tokens)
    attn_in_all = in_all.reshape(seq, width)
    query, keys, values, mixed = [a.reshape(heads, seq, size) for a in (query, keys, values, mixed)]
    log_total = lse.reshape(heads, seq, 1)
    attn = attn.transpose(1, 0, 2).reshape(rows, width)

    proj = dot(attn, out_matrix) + out_off
    mid = tokens + gate1 * proj
    normed2, rstd2 = layer_norm(mid)
    mlp_in = (normed2 * (1.0 + scale2) + shift2).astype(BF16)
    hidden = dot(mlp_in, up_matrix) + up_off
    inner = jnp.tanh(GELU_C * (hidden + CUBIC * hidden * hidden * hidden))
    act = (0.5 * hidden * (1.0 + inner)).astype(BF16)
    slope = 0.5 * (1.0 + inner) + 0.5 * hidden * (1.0 - inner * inner) * GELU_C * (
        1.0 + 3.0 * CUBIC * hidden * hidden
    )
    mlp_out = dot(act, down_matrix) + down_off
    output = mid + gate2 * mlp_out

    grad_gate2 = jnp.sum(cotangent * mlp_out, axis=0, keepdims=True)
    d_mlp = cotangent * gate2
    d_mlp16 = d_mlp.astype(BF16)
    down_term = dot_tn(act, d_mlp16)
    d_hidden = dot_nt(d_mlp16, down_matrix) * slope
    d_hidden16 = d_hidden.astype(BF16)
    up_term = dot_tn(mlp_in, d_hidden16)
    down_grad = scatter_rows(down_term, n)
    up_grad = scatter_rows(up_term, n)
    d_mlp_in = dot_nt(d_hidden16, up_matrix)
    grad_shift2 = jnp.sum(d_mlp_in, axis=0, keepdims=True)
    grad_scale2 = jnp.sum(d_mlp_in * normed2, axis=0, keepdims=True)
    d_mid = cotangent + norm_back(d_mlp_in * (1.0 + scale2), normed2, rstd2)
    grad_gate1 = jnp.sum(d_mid * proj, axis=0, keepdims=True)
    d_proj = d_mid * gate1
    d_proj16 = d_proj.astype(BF16)
    proj_grad = scatter_rows(dot_tn(attn, d_proj16), n)
    d_attn = dot_nt(d_proj16, out_matrix).astype(BF16)

    d_attn = d_attn.reshape(rows, nb, heads, size).transpose(1, 2, 0, 3)
    d_attn = lax.all_to_all(d_attn, "blk", 0, 0).transpose(1, 0, 2, 3).reshape(heads, seq, size)
    delta = jnp.sum(d_attn.astype(F32) * mixed.astype(F32), axis=-1, keepdims=True)
    scores = jnp.einsum("hqd,hkd->hqk", query, keys, preferred_element_type=F32) * scale
    probs = jnp.exp(scores - log_total)
    d_values = jnp.einsum("hqk,hqd->hkd", probs.astype(BF16), d_attn, preferred_element_type=F32)
    d_probs = jnp.einsum("hqd,hkd->hqk", d_attn, values, preferred_element_type=F32)
    d_scores = (probs * (d_probs - delta) * scale).astype(BF16)
    d_query = jnp.einsum("hqk,hkd->hqd", d_scores, keys, preferred_element_type=F32)
    d_keys = jnp.einsum("hqk,hqd->hkd", d_scores, query, preferred_element_type=F32)
    query_bias_term = jnp.sum(d_query, axis=1).reshape(local)
    value_bias_term = jnp.sum(d_values, axis=1).reshape(local)
    d_qkv = jnp.stack([d_query, d_keys, d_values]).astype(BF16)
    d_qkv = d_qkv.transpose(2, 0, 1, 3).reshape(seq, 3 * local)
    d_attn_in = dot_nt(d_qkv, qkv_cols)
    d_attn_in = lax.psum_scatter(
        d_attn_in.astype(BF16).reshape(nb, rows, width), "blk", scatter_dimension=0
    ).astype(F32)
    qkv_term = dot_tn(attn_in_all, d_qkv).astype(BF16).reshape(nl, nb * share, 3 * local)
    qkv_part = lax.psum_scatter(qkv_term, "lat", scatter_dimension=0)
    qkv_part = lax.all_to_all(qkv_part.reshape(nb, share, 3 * local), "blk", 0, 0)
    qkv_grad = qkv_part.reshape(nb, share, 3, local).transpose(1, 2, 0, 3).reshape(share, 3 * width)
    qkv_grad = qkv_grad.astype(F32)

    grad_shift1 = jnp.sum(d_attn_in, axis=0, keepdims=True)
    grad_scale1 = jnp.sum(d_attn_in * normed1, axis=0, keepdims=True)
    grad_tokens = d_mid + norm_back(d_attn_in * (1.0 + scale1), normed1, rstd1)

    zero = jnp.zeros((width,), F32)
    bias_terms = [
        lax.dynamic_update_slice(zero, query_bias_term, (my_blk * local,)),
        lax.dynamic_update_slice(zero, value_bias_term, (my_blk * local,)),
        jnp.sum(d_proj, axis=0),
        jnp.sum(d_mlp, axis=0),
        jnp.sum(d_hidden, axis=0),
    ]
    bias_term = jnp.concatenate([term.reshape(n, -1) for term in bias_terms], axis=1)
    bias_grad = lax.psum_scatter(bias_term, BOTH, scatter_dimension=0)
    cuts = [share, 2 * share, 3 * share, 4 * share]
    q_grad, v_grad, out_grad, db_grad, ub_grad = jnp.split(bias_grad, cuts)

    d_mod = jnp.concatenate(
        [grad_shift1, grad_scale1, grad_gate1, grad_shift2, grad_scale2, grad_gate2], axis=1
    )
    d_mod = lax.all_gather(lax.psum(d_mod, "blk"), "lat", axis=0, tiled=True)
    ada_grad = lax.dot_general(picked, d_mod, (((0,), (0,)), ((), ())), precision=HIGH)
    mod_total = jnp.sum(d_mod, axis=0)
    ada_bias_grad = lax.dynamic_slice(mod_total, (index * ada_bias.shape[0],), ada_bias.shape)
    back_cond = lax.dot_general(
        d_mod, ada16.astype(F32), (((1,), (1,)), ((), ())), precision=HIGH
    )
    back_cond = lax.all_gather(back_cond, BOTH, axis=0)
    back_cond = lax.dynamic_index_in_dim(back_cond, my_lat, axis=1, keepdims=False)
    grad_condition = back_cond.reshape(1, width) * silu_slope(condition)
    return (
        output[None],
        grad_tokens[None],
        grad_condition,
        ada_grad,
        ada_bias_grad,
        qkv_grad,
        q_grad,
        v_grad,
        proj_grad,
        out_grad,
        up_grad,
        ub_grad,
        down_grad,
        db_grad,
    )


def generic(
    tokens,
    condition,
    cotangent,
    ada_weight,
    ada_bias,
    qkv_weight,
    query_bias,
    value_bias,
    proj_weight,
    proj_bias,
    up_weight,
    up_bias,
    down_weight,
    down_bias,
):
    tokens, cotangent = tokens[0], cotangent[0]
    rows, width = tokens.shape
    nb, nl = lax.axis_size("blk"), lax.axis_size("lat")
    n = nb * nl
    my_lat, my_blk = lax.axis_index("lat"), lax.axis_index("blk")
    index = my_lat * nb + my_blk
    hidden_size = up_weight.shape[1]
    share = width // n
    heads = H // nb
    size = width // H
    local = heads * size
    seq = rows * nb
    scale = 1.0 / math.sqrt(size)

    cond_act = jax.nn.silu(condition)
    cond_all = lax.all_gather(cond_act, "lat", axis=0, tiled=True)
    picked = lax.dynamic_slice_in_dim(cond_all, index * share, share, axis=1)
    ada16 = ada_weight.astype(BF16)
    offset = lax.dynamic_update_slice(
        jnp.zeros((6 * width,), F32), ada_bias.astype(BF16).astype(F32), (index * ada_bias.shape[0],)
    )
    mod_part = dot(picked.astype(BF16), ada16) + offset[None, :]
    mod_part = lax.psum(mod_part, BOTH)
    modulation = lax.dynamic_slice_in_dim(mod_part, my_lat, 1, axis=0)
    shift1, scale1, gate1, shift2, scale2, gate2 = jnp.split(modulation, 6, axis=1)

    small = jnp.concatenate([query_bias, value_bias, proj_bias, down_bias, up_bias]).astype(BF16)
    small = lax.all_gather(small, BOTH, axis=0).astype(F32)
    q_off, v_off, out_off, down_off = [
        small[:, i * share : (i + 1) * share].reshape(1, width) for i in range(4)
    ]
    up_off = small[:, 4 * share :].reshape(1, hidden_size)
    q_off = lax.dynamic_slice_in_dim(q_off, my_blk * local, local, axis=1)
    v_off = lax.dynamic_slice_in_dim(v_off, my_blk * local, local, axis=1)

    cut = qkv_weight.astype(BF16).reshape(share, 3, nb, local).transpose(2, 0, 1, 3)
    cut = lax.all_to_all(cut.reshape(nb, share, 3 * local), "blk", 0, 0)
    qkv_cols = lax.all_gather(cut.reshape(nb * share, 3 * local), "lat", axis=0, tiled=True)
    out_matrix = lax.all_gather(proj_weight.astype(BF16), BOTH, axis=0, tiled=True)
    up_matrix = lax.all_gather(up_weight.astype(BF16), BOTH, axis=0, tiled=True)
    down_matrix = lax.all_gather(down_weight.astype(BF16), BOTH, axis=0, tiled=True)

    normed1, rstd1 = layer_norm(tokens)
    attn_in = (normed1 * (1.0 + scale1) + shift1).astype(BF16)
    attn_in_all = lax.all_gather(attn_in, "blk", axis=0, tiled=True)
    offsets = jnp.concatenate([q_off, jnp.zeros_like(q_off), v_off], axis=1)
    qkv = (dot(attn_in_all, qkv_cols) + offsets).astype(BF16)
    qkv = qkv.reshape(seq, 3, heads, size).transpose(1, 2, 0, 3)
    query, keys, values = qkv[0], qkv[1], qkv[2]
    scores = jnp.einsum("hqd,hkd->hqk", query, keys, preferred_element_type=F32) * scale
    peak = jnp.max(scores, axis=-1, keepdims=True)
    expo = jnp.exp(scores - peak)
    total = jnp.sum(expo, axis=-1, keepdims=True)
    accum = jnp.einsum("hqk,hkd->hqd", expo.astype(BF16), values, preferred_element_type=F32)
    log_total = peak + jnp.log(total)
    mixed = (accum / total).astype(BF16)
    back = lax.all_to_all(mixed.reshape(heads, nb, rows, size).transpose(1, 2, 0, 3), "blk", 0, 0)
    attn = back.transpose(1, 0, 2, 3).reshape(rows, width)

    proj = dot(attn, out_matrix) + out_off
    mid = tokens + gate1 * proj
    normed2, rstd2 = layer_norm(mid)
    mlp_in = (normed2 * (1.0 + scale2) + shift2).astype(BF16)
    hidden = dot(mlp_in, up_matrix) + up_off
    inner = jnp.tanh(GELU_C * (hidden + CUBIC * hidden * hidden * hidden))
    act = (0.5 * hidden * (1.0 + inner)).astype(BF16)
    slope = 0.5 * (1.0 + inner) + 0.5 * hidden * (1.0 - inner * inner) * GELU_C * (
        1.0 + 3.0 * CUBIC * hidden * hidden
    )
    mlp_out = dot(act, down_matrix) + down_off
    output = mid + gate2 * mlp_out

    grad_gate2 = jnp.sum(cotangent * mlp_out, axis=0, keepdims=True)
    d_mlp = cotangent * gate2
    d_mlp16 = d_mlp.astype(BF16)
    down_term = dot_tn(act, d_mlp16)
    d_hidden = dot_nt(d_mlp16, down_matrix) * slope
    d_hidden16 = d_hidden.astype(BF16)
    up_term = dot_tn(mlp_in, d_hidden16)
    down_grad = scatter_rows(down_term, n)
    up_grad = scatter_rows(up_term, n)
    d_mlp_in = dot_nt(d_hidden16, up_matrix)
    grad_shift2 = jnp.sum(d_mlp_in, axis=0, keepdims=True)
    grad_scale2 = jnp.sum(d_mlp_in * normed2, axis=0, keepdims=True)
    d_mid = cotangent + norm_back(d_mlp_in * (1.0 + scale2), normed2, rstd2)
    grad_gate1 = jnp.sum(d_mid * proj, axis=0, keepdims=True)
    d_proj = d_mid * gate1
    d_proj16 = d_proj.astype(BF16)
    proj_grad = scatter_rows(dot_tn(attn, d_proj16), n)
    d_attn = dot_nt(d_proj16, out_matrix).astype(BF16)

    d_attn = d_attn.reshape(rows, nb, heads, size).transpose(1, 2, 0, 3)
    d_attn = lax.all_to_all(d_attn, "blk", 0, 0).transpose(1, 0, 2, 3).reshape(heads, seq, size)
    delta = jnp.sum(d_attn.astype(F32) * mixed.astype(F32), axis=-1, keepdims=True)
    scores = jnp.einsum("hqd,hkd->hqk", query, keys, preferred_element_type=F32) * scale
    probs = jnp.exp(scores - log_total)
    d_values = jnp.einsum("hqk,hqd->hkd", probs.astype(BF16), d_attn, preferred_element_type=F32)
    d_probs = jnp.einsum("hqd,hkd->hqk", d_attn, values, preferred_element_type=F32)
    d_scores = (probs * (d_probs - delta) * scale).astype(BF16)
    d_query = jnp.einsum("hqk,hkd->hqd", d_scores, keys, preferred_element_type=F32)
    d_keys = jnp.einsum("hqk,hqd->hkd", d_scores, query, preferred_element_type=F32)
    query_bias_term = jnp.sum(d_query, axis=1).reshape(local)
    value_bias_term = jnp.sum(d_values, axis=1).reshape(local)
    d_qkv = jnp.stack([d_query, d_keys, d_values]).astype(BF16)
    d_qkv = d_qkv.transpose(2, 0, 1, 3).reshape(seq, 3 * local)
    d_attn_in = dot_nt(d_qkv, qkv_cols)
    d_attn_in = lax.psum_scatter(
        d_attn_in.astype(BF16).reshape(nb, rows, width), "blk", scatter_dimension=0
    ).astype(F32)
    qkv_term = dot_tn(attn_in_all, d_qkv).astype(BF16).reshape(nl, nb * share, 3 * local)
    qkv_part = lax.psum_scatter(qkv_term, "lat", scatter_dimension=0)
    qkv_part = lax.all_to_all(qkv_part.reshape(nb, share, 3 * local), "blk", 0, 0)
    qkv_grad = qkv_part.reshape(nb, share, 3, local).transpose(1, 2, 0, 3).reshape(share, 3 * width)
    qkv_grad = qkv_grad.astype(F32)

    grad_shift1 = jnp.sum(d_attn_in, axis=0, keepdims=True)
    grad_scale1 = jnp.sum(d_attn_in * normed1, axis=0, keepdims=True)
    grad_tokens = d_mid + norm_back(d_attn_in * (1.0 + scale1), normed1, rstd1)

    zero = jnp.zeros((width,), F32)
    bias_terms = [
        lax.dynamic_update_slice(zero, query_bias_term, (my_blk * local,)),
        lax.dynamic_update_slice(zero, value_bias_term, (my_blk * local,)),
        jnp.sum(d_proj, axis=0),
        jnp.sum(d_mlp, axis=0),
        jnp.sum(d_hidden, axis=0),
    ]
    bias_term = jnp.concatenate([term.reshape(n, -1) for term in bias_terms], axis=1)
    bias_grad = lax.psum_scatter(bias_term, BOTH, scatter_dimension=0)
    cuts = [share, 2 * share, 3 * share, 4 * share]
    q_grad, v_grad, out_grad, db_grad, ub_grad = jnp.split(bias_grad, cuts)

    d_mod = jnp.concatenate(
        [grad_shift1, grad_scale1, grad_gate1, grad_shift2, grad_scale2, grad_gate2], axis=1
    )
    d_mod = lax.all_gather(lax.psum(d_mod, "blk"), "lat", axis=0, tiled=True)
    ada_grad = lax.dot_general(picked, d_mod, (((0,), (0,)), ((), ())), precision=HIGH)
    mod_total = jnp.sum(d_mod, axis=0)
    ada_bias_grad = lax.dynamic_slice(mod_total, (index * ada_bias.shape[0],), ada_bias.shape)
    back_cond = lax.dot_general(
        d_mod, ada16.astype(F32), (((1,), (1,)), ((), ())), precision=HIGH
    )
    back_cond = lax.all_gather(back_cond, BOTH, axis=0)
    back_cond = lax.dynamic_index_in_dim(back_cond, my_lat, axis=1, keepdims=False)
    grad_condition = back_cond.reshape(1, width) * silu_slope(condition)
    return (
        output[None],
        grad_tokens[None],
        grad_condition,
        ada_grad,
        ada_bias_grad,
        qkv_grad,
        q_grad,
        v_grad,
        proj_grad,
        out_grad,
        up_grad,
        ub_grad,
        down_grad,
        db_grad,
    )


def solution(mesh):
    rows, vec = P(BOTH, None), P(BOTH)
    tok, cond = P("lat", "blk", None), P("lat", None)
    in_specs = (tok, cond, tok, rows, vec, rows, vec, vec, rows, vec, rows, vec, rows, vec)
    out_specs = (tok, tok, cond, rows, vec, rows, vec, vec, rows, vec, rows, vec, rows, vec)
    body = fused if mesh.shape["lat"] == 8 and mesh.shape["blk"] == 4 else generic
    return jax.shard_map(body, mesh=mesh, in_specs=in_specs, out_specs=out_specs, check_vma=False)
```
